32 devices in a mesh: dp: 4 (over y, x), expert: 8 (over z, core).
Axes of the slice: x: 2, y: 2, z: 4, core: 2. Of those that a mesh axis runs over, the one named last changes fastest.
Arguments:
- tokens: bfloat16 [4096, 2048], P(('dp', 'expert')), may hold values from -6 to 6
- cotangent: bfloat16 [4096, 2048], P(('dp', 'expert')), may hold values from -1.5 to 1.5
- expert_ids: int32 [4096, 8], P(('dp', 'expert')), may hold values from 0 to 127, as said below
- gate_values: float32 [4096, 8], P(('dp', 'expert')), may hold values from 0.1 to 0.5
- w_gate: bfloat16 [2048, 8, 768], P(None, 'expert'), may hold values from -0.125 to 0.125
- w_up: bfloat16 [2048, 8, 768], P(None, 'expert'), may hold values from -0.125 to 0.125
- w_down: bfloat16 [2048, 8, 768], P(None, 'expert'), may hold values from -0.21875 to 0.21875
Outputs:
- output: bfloat16 [4096, 2048], P(('dp', 'expert'))
- grad_input: bfloat16 [4096, 2048], P(('dp', 'expert'))
- grad_gate: float32 [2048, 8, 768], P('dp', 'expert')
- grad_up: float32 [2048, 8, 768], P('dp', 'expert')
- grad_down: float32 [2048, 8, 768], P('dp', 'expert')
The draws below stay inside these ranges and needn't reach their ends.
Inputs may be any that keep to these rules, and one draw needn't show every extreme that they name: `expert_ids`: each row names 8 different experts in any order. In the rows of one device no expert under 8 is named more than 32 times; in each group of 1024 rows (one index of dp) one expert under 8 is named exactly 32 times by the rows of every device of the group.
All inputs are finite; a program needn't handle non-finite values.
Results may differ from the reference program's by a relative error of at most 0.013.
Values may be sent and summed in bfloat16 or wider, within the bound.
A program may use at most 128 MiB of HBM per device.

```python
import jax
import jax.numpy as jnp
from jax import lax

D = 2048
FW = 768
TOPK = 8
EXPERTS_ALL = 128
TOK_DEV = 128
CAP = 32
EXPERTS = 8
GROUP_TOK = 1024
TOKENS = 4096
N_EXPERT = 8


def draw_expert_ids(key, part):
    key_hot, key_pick, key_rot, key_second, key_outer, key_order = jax.random.split(key, 6)
    blocks = TOKENS // TOK_DEV
    groups = TOKENS // GROUP_TOK
    hot = jax.random.randint(key_hot, (groups,), 0, EXPERTS).astype(jnp.int32)
    block_group = jnp.arange(blocks, dtype=jnp.int32) // (GROUP_TOK // TOK_DEV)
    hot_block = hot[block_group][:, None]
    local_range = jnp.arange(TOK_DEV, dtype=jnp.int32)
    pick_score = jax.random.randint(key_pick, (blocks, TOK_DEV), 0, 1 << 20) * TOK_DEV + local_range[None, :]
    position = jnp.argsort(jnp.argsort(pick_score, axis=1, stable=True), axis=1, stable=True).astype(jnp.int32)
    takes_hot = position < CAP
    rotation = jax.random.randint(key_rot, (blocks, 1), 0, EXPERTS - 1).astype(jnp.int32)
    other_index = (position + rotation) % (EXPERTS - 1)
    other_expert = other_index + (other_index >= hot_block).astype(jnp.int32)
    has_second = jax.random.randint(key_second, (blocks, TOK_DEV), 0, 4) > 0
    outside_count = EXPERTS_ALL - EXPERTS
    outer_score = jax.random.randint(key_outer, (TOKENS, outside_count), 0, 1 << 20) * outside_count + jnp.arange(outside_count, dtype=jnp.int32)[None, :]
    outer_values, outer_picked = lax.top_k(outer_score, TOPK)
    outer_ids = outer_picked.astype(jnp.int32).reshape(blocks, TOK_DEV, TOPK) + EXPERTS
    first = jnp.where(takes_hot, hot_block, outer_ids[:, :, 0])
    second = jnp.where(has_second, other_expert, outer_ids[:, :, 1])
    columns = jnp.concatenate((first[:, :, None], second[:, :, None], outer_ids[:, :, 2:]), axis=2)
    columns = columns.reshape(TOKENS, TOPK)
    order_score = jax.random.randint(key_order, (TOKENS, TOPK), 0, 1 << 20) * TOPK + jnp.arange(TOPK, dtype=jnp.int32)[None, :]
    order = jnp.argsort(order_score, axis=1, stable=True)
    return jnp.take_along_axis(columns, order, axis=1).astype(jnp.int32)


def steps_of(key, dims, cuts, smallest, largest):
    factor_of = 1.0
    for axis_at, blocks in cuts:
        draws = jax.random.uniform(jax.random.fold_in(jax.random.fold_in(key, 6), axis_at), (blocks,), jnp.float32, smallest / len(cuts), largest / len(cuts))
        factor_of = factor_of * jnp.repeat(jnp.exp(draws), dims[axis_at] // blocks).reshape((-1,) + (1,) * (len(dims) - 1 - axis_at))
    return factor_of


def bell_draw(stream_key, extent, deviation, reach, cuts=(), held_as=jnp.bfloat16):
    drawn = deviation * jax.random.normal(stream_key, extent, jnp.float32)
    if cuts:
        drawn = drawn * steps_of(stream_key, extent, cuts, -0.22, 0.18)
    return jnp.clip(drawn, -reach, reach).astype(held_as)


def setup_inputs(seed: int = 0) -> dict:
    key_of = jax.random.split(jax.random.key(seed), 8)
    return {
        "tokens": bell_draw(key_of[0], (TOKENS, D), 1.0, 6.0, ((0, 32),)),
        "cotangent": bell_draw(key_of[1], (TOKENS, D), 0.25, 1.5, ((0, 32),)),
        "expert_ids": draw_expert_ids(jax.random.fold_in(key_of[7], 71), 0),
        "gate_values": jnp.clip(0.1 + 0.4 * jax.random.uniform(key_of[3], (TOKENS, TOPK), jnp.float32) ** steps_of(key_of[3], (TOKENS, TOPK), ((0, 32),), -0.2, 0.2), 0.1, 0.5),
        "w_gate": bell_draw(key_of[4], (D, EXPERTS, FW), D ** -0.5, 0.125, ((1, 8),)),
        "w_up": bell_draw(key_of[5], (D, EXPERTS, FW), D ** -0.5, 0.125, ((1, 8),)),
        "w_down": bell_draw(key_of[6], (D, EXPERTS, FW), FW ** -0.5, 0.21875, ((1, 8),)),
    }


def reference(tokens, cotangent, expert_ids, gate_values, w_gate, w_up, w_down):
    blocks = tokens.shape[0] // TOK_DEV
    groups = blocks // N_EXPERT
    experts_all = w_gate.shape[1]
    x_blocks = tokens.reshape(blocks, TOK_DEV, D).astype(jnp.float32)
    dy_blocks = cotangent.reshape(blocks, TOK_DEV, D).astype(jnp.float32)
    ids = expert_ids.reshape(blocks, TOK_DEV, TOPK)
    gates = gate_values.reshape(blocks, TOK_DEV, TOPK)
    expert_range = jnp.arange(experts_all, dtype=jnp.int32)
    chosen = (ids[..., None] == expert_range).astype(jnp.int32)
    present = jnp.sum(chosen, axis=2, dtype=jnp.int32)
    earlier = jnp.cumsum(present, axis=1, dtype=jnp.int32) - present
    weight_of = jnp.sum(chosen.astype(jnp.float32) * gates[..., None], axis=2)
    slot_range = jnp.arange(CAP, dtype=jnp.int32)
    highest = lax.Precision.HIGHEST

    def group_sum(left, right):
        left_g = left.reshape(groups, -1, left.shape[-1]).astype(jnp.float32)
        right_g = right.reshape(groups, -1, right.shape[-1]).astype(jnp.float32)
        partial_value = jnp.einsum("grd,grf->gdf", left_g, right_g, precision=highest).astype(jnp.bfloat16)
        partial_value = lax.optimization_barrier(partial_value)
        return jnp.sum(partial_value.astype(jnp.float32), axis=0)

    def one_expert(carry, expert):
        total_out, total_dx = carry
        here = lax.dynamic_index_in_dim(present, expert, 2, keepdims=False)
        rank_here = lax.dynamic_index_in_dim(earlier, expert, 2, keepdims=False)
        gate_here = lax.dynamic_index_in_dim(weight_of, expert, 2, keepdims=False)
        place = ((rank_here[:, :, None] == slot_range[None, None, :]) & (here[:, :, None] > 0)).astype(jnp.float32)
        weighted = place * gate_here[:, :, None]
        x_slots = jnp.einsum("btc,btd->bcd", place, x_blocks, precision=highest).astype(jnp.bfloat16)
        z_slots = jnp.einsum("btc,btd->bcd", weighted, dy_blocks, precision=highest).astype(jnp.bfloat16)
        x_rows = x_slots.reshape(-1, D)
        z_rows = z_slots.reshape(-1, D)
        wg = lax.dynamic_index_in_dim(w_gate, expert, 1, keepdims=False)
        wu = lax.dynamic_index_in_dim(w_up, expert, 1, keepdims=False)
        wd = lax.dynamic_index_in_dim(w_down, expert, 1, keepdims=False)
        gate_pre = jnp.dot(x_rows, wg, preferred_element_type=jnp.float32)
        up_pre = jnp.dot(x_rows, wu, preferred_element_type=jnp.float32)
        sig = jax.nn.sigmoid(gate_pre)
        hidden = (gate_pre * sig * up_pre).astype(jnp.bfloat16)
        slot_out = jnp.dot(hidden, wd.T, preferred_element_type=jnp.float32).astype(jnp.bfloat16)
        d_hidden = jnp.dot(z_rows, wd, preferred_element_type=jnp.float32)
        d_gate = (d_hidden * up_pre * sig * (1.0 + gate_pre * (1.0 - sig))).astype(jnp.bfloat16)
        d_up = (d_hidden * gate_pre * sig).astype(jnp.bfloat16)
        slot_dx = (jnp.dot(d_gate, wg.T, preferred_element_type=jnp.float32)
                   + jnp.dot(d_up, wu.T, preferred_element_type=jnp.float32)).astype(jnp.bfloat16)
        grad_g = group_sum(x_rows, d_gate)
        grad_u = group_sum(x_rows, d_up)
        grad_d = group_sum(z_rows, hidden)
        out_blocks = slot_out.reshape(blocks, CAP, D).astype(jnp.float32)
        dx_blocks = slot_dx.reshape(blocks, CAP, D).astype(jnp.float32)
        total_out = total_out + jnp.einsum("btc,bcd->btd", weighted, out_blocks, precision=highest)
        total_dx = total_dx + jnp.einsum("btc,bcd->btd", place, dx_blocks, precision=highest)
        return (total_out, total_dx), (grad_g, grad_u, grad_d)

    start = (jnp.zeros((blocks, TOK_DEV, D), jnp.float32), jnp.zeros((blocks, TOK_DEV, D), jnp.float32))
    (total_out, total_dx), (grad_g, grad_u, grad_d) = lax.scan(one_expert, start, expert_range)
    output = total_out.reshape(-1, D).astype(jnp.bfloat16)
    grad_input = total_dx.reshape(-1, D).astype(jnp.bfloat16)
    return (output, grad_input, jnp.transpose(grad_g, (1, 0, 2)), jnp.transpose(grad_u, (1, 0, 2)),
            jnp.transpose(grad_d, (1, 0, 2)))
```

```python
import functools

import jax
import jax.numpy as jnp
from jax import lax
from jax.experimental import pallas as pl
from jax.experimental.pallas import tpu as pltpu
from jax.sharding import PartitionSpec as P

MESH = pl.DeviceIdType.MESH
F32 = jnp.float32
BF16 = jnp.bfloat16


def dot(a, b, dims=((1,), (0,))):
    return lax.dot_general(a, b, (dims, ((), ())), preferred_element_type=F32)


def tile_of(size):
    return 256 if size % 256 == 0 else 128


def kernel(
    owners, groups, cap,
    tokens, cotangent, ids, gates, wg_hbm, wu_hbm, wd_hbm,
    output, grad_input, x_cols, z_cols, hid_all, dg_all, du_all,
    wg, wu, wd, x_send, z_send, x_rows, z_rows, out_send, dx_send, out_back, dx_back,
    hid, dg, du, gate_pre, up_pre, sel, gate_hi, gate_lo,
    w_sem, self_sem, own_sem,
    x_ss, x_rs, z_ss, z_rs, o_ss, o_rs, d_ss, d_rs,
    c_ss, c_rs,
):
    me = lax.axis_index("expert")
    my_dp = lax.axis_index("dp")
    toks, width = tokens.shape
    slots = owners * cap
    hidden_units = hid.shape[1]
    cols = width // groups

    loads = [
        pltpu.make_async_copy(src, dst, w_sem.at[i])
        for i, (src, dst) in enumerate(((wg_hbm, wg), (wu_hbm, wu), (wd_hbm, wd)))
    ]
    for load in loads:
        load.start()

    barrier = pltpu.get_barrier_semaphore()
    for i in range(1, owners):
        pl.semaphore_signal(
            barrier, inc=1, device_id={"expert": lax.rem(me + i, owners)}, device_id_type=MESH
        )
    for i in range(1, groups):
        pl.semaphore_signal(
            barrier, inc=1, device_id={"dp": lax.rem(my_dp + i, groups)}, device_id_type=MESH
        )

    lanes = 128
    expert = lax.broadcasted_iota(jnp.int32, (toks, lanes), 1)
    present = jnp.zeros((toks, lanes), F32)
    gate = jnp.zeros((toks, lanes), F32)
    for k in range(ids.shape[1]):
        hit = ids[:, k : k + 1] == expert
        present = jnp.where(hit, 1.0, present)
        gate = jnp.where(hit, gates[:, k : k + 1], gate)
    row = lax.broadcasted_iota(jnp.int32, (toks, toks), 0)
    col = lax.broadcasted_iota(jnp.int32, (toks, toks), 1)
    before = jnp.where(col < row, 1.0, 0.0).astype(BF16)
    rank = dot(before, present.astype(BF16))
    rank = jnp.where(present > 0.0, rank, -1.0)
    spread = jnp.where(
        lax.broadcasted_iota(jnp.int32, (lanes, slots), 1) // cap
        == lax.broadcasted_iota(jnp.int32, (lanes, slots), 0),
        1.0,
        0.0,
    ).astype(BF16)
    rank_at = dot(rank.astype(BF16), spread)
    place = lax.rem(lax.broadcasted_iota(jnp.int32, (toks, slots), 1), cap).astype(F32)
    chosen = jnp.where(rank_at == place, 1.0, 0.0)
    hi = gate.astype(BF16)
    lo = (gate - hi.astype(F32)).astype(BF16)
    hi_at = dot(hi, spread) * chosen
    lo_at = dot(lo, spread) * chosen
    sel[...] = chosen.astype(BF16)
    gate_hi[...] = hi_at.astype(BF16)
    gate_lo[...] = lo_at.astype(BF16)
    sel_t = chosen.T.astype(BF16)
    hi_t = hi_at.T.astype(BF16)
    lo_t = lo_at.T.astype(BF16)
    dt = tile_of(width)

    @pl.loop(0, width // dt)
    def _(i):
        at = pl.ds(pl.multiple_of(i * dt, dt), dt)
        x_send[:, at] = dot(sel_t, tokens[:, at]).astype(BF16)

    def block(r):
        return pl.ds(pl.multiple_of(r * cap, cap), cap)

    def exchange(src, dst, ss, rs, own):
        copies = [pltpu.make_async_copy(src.at[block(me), :], dst.at[block(me), :], own)]
        for i in range(1, owners):
            peer = lax.rem(me + i, owners)
            copies.append(
                pltpu.make_async_remote_copy(
                    src_ref=src.at[block(peer), :],
                    dst_ref=dst.at[block(me), :],
                    send_sem=ss.at[i - 1],
                    recv_sem=rs.at[i - 1],
                    device_id={"expert": peer},
                    device_id_type=MESH,
                )
            )
        for c in copies:
            c.start()
        return copies

    def share(n, src_of, dst):
        copies = [pltpu.make_async_copy(src_of(my_dp), dst.at[my_dp], own_sem.at[n])]
        for i in range(1, groups):
            peer = lax.rem(my_dp + i, groups)
            copies.append(
                pltpu.make_async_remote_copy(
                    src_ref=src_of(peer),
                    dst_ref=dst.at[my_dp],
                    send_sem=c_ss.at[n, i - 1],
                    recv_sem=c_rs.at[n, i - 1],
                    device_id={"dp": peer},
                    device_id_type=MESH,
                )
            )
        for c in copies:
            c.start()
        return copies

    def finish(copies):
        for c in copies:
            c.wait()

    def columns(ref):
        return lambda g: ref.at[:, pl.ds(pl.multiple_of(g * cols, cols), cols)]

    pl.semaphore_wait(barrier, owners + groups - 2)
    x_copies = exchange(x_send, x_rows, x_ss, x_rs, self_sem.at[0])

    @pl.loop(0, width // dt)
    def _(i):
        at = pl.ds(pl.multiple_of(i * dt, dt), dt)
        c = cotangent[:, at]
        z_send[:, at] = (dot(hi_t, c) + dot(lo_t, c)).astype(BF16)

    z_copies = exchange(z_send, z_rows, z_ss, z_rs, self_sem.at[1])

    finish(loads)
    finish(x_copies)
    shared = share(0, columns(x_rows), x_cols)

    ft = tile_of(hidden_units)

    @pl.loop(0, hidden_units // ft)
    def _(i):
        at = pl.ds(pl.multiple_of(i * ft, ft), ft)
        g = dot(x_rows[...], wg[:, at])
        u = dot(x_rows[...], wu[:, at])
        gate_pre[:, at] = g
        up_pre[:, at] = u
        hid[:, at] = (g * lax.logistic(g) * u).astype(BF16)

    shared += share(1, lambda g: hid, hid_all)

    @pl.loop(0, width // dt)
    def _(i):
        at = pl.ds(pl.multiple_of(i * dt, dt), dt)
        out_send[:, at] = dot(hid[...], wd[at, :], ((1,), (1,))).astype(BF16)

    finish(z_copies)
    shared += share(2, columns(z_rows), z_cols)
    o_copies = exchange(out_send, out_back, o_ss, o_rs, self_sem.at[2])

    @pl.loop(0, hidden_units // ft)
    def _(i):
        at = pl.ds(pl.multiple_of(i * ft, ft), ft)
        dh = dot(z_rows[...], wd[:, at])
        g = gate_pre[:, at]
        s = lax.logistic(g)
        dg[:, at] = (dh * up_pre[:, at] * s * (1.0 + g * (1.0 - s))).astype(BF16)
        du[:, at] = (dh * g * s).astype(BF16)

    shared += share(3, lambda g: dg, dg_all)
    shared += share(4, lambda g: du, du_all)

    @pl.loop(0, width // dt)
    def _(i):
        at = pl.ds(pl.multiple_of(i * dt, dt), dt)
        dx_send[:, at] = (
            dot(dg[...], wg[at, :], ((1,), (1,))) + dot(du[...], wu[at, :], ((1,), (1,)))
        ).astype(BF16)

    d_copies = exchange(dx_send, dx_back, d_ss, d_rs, self_sem.at[3])

    finish(o_copies)

    @pl.loop(0, width // dt)
    def _(i):
        at = pl.ds(pl.multiple_of(i * dt, dt), dt)
        r = out_back[:, at]
        output[:, at] = (dot(gate_hi[...], r) + dot(gate_lo[...], r)).astype(BF16)

    finish(d_copies)

    @pl.loop(0, width // dt)
    def _(i):
        at = pl.ds(pl.multiple_of(i * dt, dt), dt)
        grad_input[:, at] = dot(sel[...], dx_back[:, at]).astype(BF16)

    finish(shared)


def per_device(tokens, cotangent, expert_ids, gate_values, w_gate, w_up, w_down):
    owners = lax.axis_size("expert")
    groups = lax.axis_size("dp")
    toks, width = tokens.shape
    cap = toks // 4
    local, units = w_gate.shape[1:]
    assert local == 1
    slots = owners * cap
    cols = width // groups
    vmem = pl.BlockSpec(memory_space=pltpu.VMEM)
    hbm = pl.BlockSpec(memory_space=pl.ANY)
    rows = pltpu.VMEM((slots, width), BF16)
    acts = pltpu.VMEM((slots, units), BF16)
    weight = pltpu.VMEM((width, units), BF16)
    wide = pltpu.VMEM((slots, units), F32)
    table = pltpu.VMEM((toks, slots), BF16)
    dma = pltpu.SemaphoreType.DMA
    out, dx, x_cols, z_cols, hid, dg, du = pl.pallas_call(
        functools.partial(kernel, owners, groups, cap),
        out_shape=[jax.ShapeDtypeStruct((toks, width), BF16)] * 2
        + [jax.ShapeDtypeStruct((groups, slots, cols), BF16)] * 2
        + [jax.ShapeDtypeStruct((groups, slots, units), BF16)] * 3,
        in_specs=[vmem] * 4 + [hbm] * 3,
        out_specs=[vmem] * 2 + [hbm] * 5,
        scratch_shapes=[weight] * 3
        + [rows] * 8
        + [acts] * 3
        + [wide] * 2
        + [table] * 3
        + [dma((3,)), dma((4,)), dma((5,))]
        + [dma((owners - 1,))] * 8
        + [dma((5, groups - 1))] * 2,
        compiler_params=pltpu.CompilerParams(
            collective_id=0, has_side_effects=True, vmem_limit_bytes=50 * 2**20
        ),
        name="moe",
    )(
        tokens, cotangent, expert_ids, gate_values,
        w_gate[:, 0], w_up[:, 0], w_down[:, 0],
    )

    def grad(a, b):
        return jnp.einsum("gsd,gsf->df", a, b, preferred_element_type=F32)[:, None, :]

    return out, dx, grad(x_cols, dg), grad(x_cols, du), grad(z_cols, hid)


def solution(mesh):
    rows = P(("dp", "expert"), None)
    held = P(None, "expert", None)
    grads = P("dp", "expert", None)
    return jax.shard_map(
        per_device,
        mesh=mesh,
        in_specs=(rows, rows, rows, rows, held, held, held),
        out_specs=(rows, rows, grads, grads, grads),
        check_vma=False,
    )
```

```python
import functools

import jax
import jax.numpy as jnp
from jax import lax
from jax.experimental import pallas as pl
from jax.experimental.pallas import tpu as pltpu
from jax.sharding import PartitionSpec as P

MESH = pl.DeviceIdType.MESH
F32 = jnp.float32
BF16 = jnp.bfloat16


def dot(a, b, dims=((1,), (0,))):
    return lax.dot_general(a, b, (dims, ((), ())), preferred_element_type=F32)


def tile_of(size):
    return 256 if size % 256 == 0 else 128


def kernel(
    owners, groups, cap,
    tok_hbm, cot_hbm, ids, gates, wg_hbm, wu_hbm, wd_hbm,
    output, grad_input, x_cols, z_cols, hid_all, dg_all, du_all,
    tokens, cotangent, wg, wu, wd, x_send, z_send, x_rows, z_rows, out_send, dx_send, out_back, dx_back,
    hid, dg, du, gate_pre, up_pre, sel, gate_hi, gate_lo,
    w_sem, self_sem, own_sem,
    x_ss, x_rs, z_ss, z_rs, o_ss, o_rs, d_ss, d_rs,
    c_ss, c_rs,
):
    me = lax.axis_index("expert")
    my_dp = lax.axis_index("dp")
    toks, width = tokens.shape
    slots = owners * cap
    hidden_units = hid.shape[1]
    cols = width // groups

    loads = [
        pltpu.make_async_copy(src, dst, w_sem.at[i])
        for i, (src, dst) in enumerate(
            (
                (tok_hbm, tokens),
                (cot_hbm, cotangent),
                (wg_hbm, wg),
                (wu_hbm, wu),
                (wd_hbm, wd),
            )
        )
    ]
    for load in loads:
        load.start()

    barrier = pltpu.get_barrier_semaphore()
    for i in range(1, owners):
        pl.semaphore_signal(
            barrier, inc=1, device_id={"expert": lax.rem(me + i, owners)}, device_id_type=MESH
        )
    for i in range(1, groups):
        pl.semaphore_signal(
            barrier, inc=1, device_id={"dp": lax.rem(my_dp + i, groups)}, device_id_type=MESH
        )

    lanes = 128
    expert = lax.broadcasted_iota(jnp.int32, (lanes, toks), 0)
    present = jnp.zeros((lanes, toks), F32)
    gate = jnp.zeros((lanes, toks), F32)
    for k in range(ids.shape[0]):
        hit = ids[k : k + 1, :] == expert
        present = jnp.where(hit, 1.0, present)
        gate = jnp.where(hit, gates[k : k + 1, :], gate)
    row = lax.broadcasted_iota(jnp.int32, (toks, toks), 0)
    col = lax.broadcasted_iota(jnp.int32, (toks, toks), 1)
    before = jnp.where(row < col, 1.0, 0.0).astype(BF16)
    rank = dot(present.astype(BF16), before)
    rank = jnp.where(present > 0.0, rank, -1.0)
    spread = jnp.where(
        lax.broadcasted_iota(jnp.int32, (slots, lanes), 0) // cap
        == lax.broadcasted_iota(jnp.int32, (slots, lanes), 1),
        1.0,
        0.0,
    ).astype(BF16)
    rank_at = dot(spread, rank.astype(BF16))
    place = lax.rem(lax.broadcasted_iota(jnp.int32, (slots, toks), 0), cap).astype(F32)
    chosen = jnp.where(rank_at == place, 1.0, 0.0)
    hi = gate.astype(BF16)
    lo = (gate - hi.astype(F32)).astype(BF16)
    hi_at = dot(spread, hi) * chosen
    lo_at = dot(spread, lo) * chosen
    sel_t = chosen.astype(BF16)
    hi_t = hi_at.astype(BF16)
    lo_t = lo_at.astype(BF16)
    dt = tile_of(width)

    loads[0].wait()

    @pl.loop(0, width // dt)
    def _(i):
        at = pl.ds(pl.multiple_of(i * dt, dt), dt)
        x_send[:, at] = dot(sel_t, tokens[:, at]).astype(BF16)

    def block(r):
        return pl.ds(pl.multiple_of(r * cap, cap), cap)

    def exchange(src, dst, ss, rs, own):
        copies = [pltpu.make_async_copy(src.at[block(me), :], dst.at[block(me), :], own)]
        half = owners // 2
        side, spot = me // half, lax.rem(me, half)
        peers = [(1 - side) * half + lax.rem(spot + i, half) for i in range(half)]
        peers += [side * half + lax.rem(spot + i, half) for i in range(1, half)]
        for i, peer in enumerate(peers, 1):
            copies.append(
                pltpu.make_async_remote_copy(
                    src_ref=src.at[block(peer), :],
                    dst_ref=dst.at[block(me), :],
                    send_sem=ss.at[i - 1],
                    recv_sem=rs.at[i - 1],
                    device_id={"expert": peer},
                    device_id_type=MESH,
                )
            )
        for c in copies:
            c.start()
        return copies

    def share(n, src_of, dst):
        copies = [pltpu.make_async_copy(src_of(my_dp), dst.at[my_dp], own_sem.at[n])]
        for i in range(1, groups):
            peer = lax.rem(my_dp + i, groups)
            copies.append(
                pltpu.make_async_remote_copy(
                    src_ref=src_of(peer),
                    dst_ref=dst.at[my_dp],
                    send_sem=c_ss.at[n, i - 1],
                    recv_sem=c_rs.at[n, i - 1],
                    device_id={"dp": peer},
                    device_id_type=MESH,
                )
            )
        for c in copies:
            c.start()
        return copies

    def finish(copies):
        for c in copies:
            c.wait()

    def columns(ref):
        return lambda g: ref.at[:, pl.ds(pl.multiple_of(g * cols, cols), cols)]

    pl.semaphore_wait(barrier, owners + groups - 2)
    x_copies = exchange(x_send, x_rows, x_ss, x_rs, self_sem.at[0])

    loads[1].wait()

    @pl.loop(0, width // dt)
    def _(i):
        at = pl.ds(pl.multiple_of(i * dt, dt), dt)
        c = cotangent[:, at]
        z_send[:, at] = (dot(hi_t, c) + dot(lo_t, c)).astype(BF16)

    z_copies = exchange(z_send, z_rows, z_ss, z_rs, self_sem.at[1])

    sel[...] = chosen.T.astype(BF16)
    gate_hi[...] = hi_at.T.astype(BF16)
    gate_lo[...] = lo_at.T.astype(BF16)
    finish(loads[2:])
    finish(x_copies)
    shared = share(0, columns(x_rows), x_cols)

    ft = tile_of(hidden_units)

    @pl.loop(0, hidden_units // ft)
    def _(i):
        at = pl.ds(pl.multiple_of(i * ft, ft), ft)
        g = dot(x_rows[...], wg[:, at])
        u = dot(x_rows[...], wu[:, at])
        gate_pre[:, at] = g
        up_pre[:, at] = u
        hid[:, at] = (g * lax.logistic(g) * u).astype(BF16)

    shared += share(1, lambda g: hid, hid_all)

    @pl.loop(0, width // dt)
    def _(i):
        at = pl.ds(pl.multiple_of(i * dt, dt), dt)
        out_send[:, at] = dot(hid[...], wd[at, :], ((1,), (1,))).astype(BF16)

    finish(z_copies)
    shared += share(2, columns(z_rows), z_cols)
    o_copies = exchange(out_send, out_back, o_ss, o_rs, self_sem.at[2])

    @pl.loop(0, hidden_units // ft)
    def _(i):
        at = pl.ds(pl.multiple_of(i * ft, ft), ft)
        dh = dot(z_rows[...], wd[:, at])
        g = gate_pre[:, at]
        s = lax.logistic(g)
        dg[:, at] = (dh * up_pre[:, at] * s * (1.0 + g * (1.0 - s))).astype(BF16)
        du[:, at] = (dh * g * s).astype(BF16)

    shared += share(3, lambda g: dg, dg_all)
    shared += share(4, lambda g: du, du_all)

    @pl.loop(0, width // dt)
    def _(i):
        at = pl.ds(pl.multiple_of(i * dt, dt), dt)
        dx_send[:, at] = (
            dot(dg[...], wg[at, :], ((1,), (1,))) + dot(du[...], wu[at, :], ((1,), (1,)))
        ).astype(BF16)

    d_copies = exchange(dx_send, dx_back, d_ss, d_rs, self_sem.at[3])

    finish(o_copies)

    @pl.loop(0, width // dt)
    def _(i):
        at = pl.ds(pl.multiple_of(i * dt, dt), dt)
        r = out_back[:, at]
        output[:, at] = (dot(gate_hi[...], r) + dot(gate_lo[...], r)).astype(BF16)

    finish(d_copies)

    @pl.loop(0, width // dt)
    def _(i):
        at = pl.ds(pl.multiple_of(i * dt, dt), dt)
        grad_input[:, at] = dot(sel[...], dx_back[:, at]).astype(BF16)

    finish(shared)


def weight_grads(
    out_in, dx_in, x_in, z_in, dg_in, du_in, hid_in,
    out, dx, grad_gate, grad_up, grad_down,
    x, z, dg, du, hid, panel_gate, panel_up, panel_down, in_sem, out_sem,
):
    loads = [
        pltpu.make_async_copy(a, b, in_sem.at[i])
        for i, (a, b) in enumerate(
            ((x_in, x), (dg_in, dg), (du_in, du), (z_in, z), (hid_in, hid))
        )
    ]
    stores = [
        pltpu.make_async_copy(a, b, out_sem.at[i])
        for i, (a, b) in enumerate(
            (
                (out_in, out),
                (dx_in, dx),
                (panel_gate, grad_gate),
                (panel_up, grad_up),
                (panel_down, grad_down),
            )
        )
    ]
    for c in loads + stores[:2]:
        c.start()
    cols, units = x.shape[1], dg.shape[1]
    lines = units // 128
    ft = tile_of(units)
    for n, (a, b, panel, needs) in enumerate(
        (
            (x, dg, panel_gate, loads[:2]),
            (x, du, panel_up, loads[2:3]),
            (z, hid, panel_down, loads[3:]),
        )
    ):
        for c in needs:
            c.wait()
        for f in range(0, units, ft):
            total = dot(a[...], b[:, f : f + ft], ((0,), (0,)))
            for j in range(ft // 128):
                panel[pl.ds(f // 128 + j, cols, stride=lines), :] = total[
                    :, j * 128 : (j + 1) * 128
                ]
        stores[2 + n].start()
    for c in stores:
        c.wait()


def per_device(tokens, cotangent, expert_ids, gate_values, w_gate, w_up, w_down):
    owners = lax.axis_size("expert")
    groups = lax.axis_size("dp")
    toks, width = tokens.shape
    cap = toks // 4
    local, units = w_gate.shape[1:]
    assert local == 1
    slots = owners * cap
    cols = width // groups
    vmem = pl.BlockSpec(memory_space=pltpu.VMEM)
    hbm = pl.BlockSpec(memory_space=pl.ANY)
    rows = pltpu.VMEM((slots, width), BF16)
    acts = pltpu.VMEM((slots, units), BF16)
    weight = pltpu.VMEM((width, units), BF16)
    wide = pltpu.VMEM((slots, units), F32)
    table = pltpu.VMEM((toks, slots), BF16)
    dma = pltpu.SemaphoreType.DMA
    out, dx, x_cols, z_cols, hid, dg, du = pl.pallas_call(
        functools.partial(kernel, owners, groups, cap),
        out_shape=[jax.ShapeDtypeStruct((toks, width), BF16)] * 2
        + [jax.ShapeDtypeStruct((groups, slots, cols), BF16)] * 2
        + [jax.ShapeDtypeStruct((groups, slots, units), BF16)] * 3,
        in_specs=[hbm] * 2 + [vmem] * 2 + [hbm] * 3,
        out_specs=[vmem] * 2 + [hbm] * 5,
        scratch_shapes=[pltpu.VMEM((toks, width), BF16)] * 2
        + [weight] * 3
        + [rows] * 8
        + [acts] * 3
        + [wide] * 2
        + [table] * 3
        + [dma((5,)), dma((4,)), dma((5,))]
        + [dma((owners - 1,))] * 8
        + [dma((5, groups - 1))] * 2,
        compiler_params=pltpu.CompilerParams(
            collective_id=0, has_side_effects=True, vmem_limit_bytes=58 * 2**20
        ),
        name="moe",
    )(
        tokens, cotangent, expert_ids.T, gate_values.T,
        w_gate[:, 0], w_up[:, 0], w_down[:, 0],
    )

    flat = [a.reshape(groups * slots, -1) for a in (x_cols, z_cols, dg, du, hid)]
    lines = units // 128
    panel = jax.ShapeDtypeStruct((cols * lines, 128), F32)
    out, dx, *panels = pl.pallas_call(
        weight_grads,
        out_shape=[jax.ShapeDtypeStruct((toks, width), BF16)] * 2 + [panel] * 3,
        in_specs=[hbm] * 7,
        out_specs=[hbm] * 5,
        scratch_shapes=[pltpu.VMEM(a.shape, BF16) for a in flat]
        + [pltpu.VMEM(panel.shape, F32)] * 3
        + [dma((5,)), dma((5,))],
        compiler_params=pltpu.CompilerParams(vmem_limit_bytes=58 * 2**20),
        name="weight_grads",
    )(out, dx, *flat)
    return out, dx, *(p.reshape(cols, 1, units) for p in panels)


def solution(mesh):
    rows = P(("dp", "expert"), None)
    held = P(None, "expert", None)
    grads = P("dp", "expert", None)
    return jax.shard_map(
        per_device,
        mesh=mesh,
        in_specs=(rows, rows, rows, rows, held, held, held),
        out_specs=(rows, rows, grads, grads, grads),
        check_vma=False,
    )
```

```python
import functools

import jax
import jax.numpy as jnp
from jax import lax
from jax.experimental import pallas as pl
from jax.experimental.pallas import tpu as pltpu
from jax.sharding import PartitionSpec as P

MESH = pl.DeviceIdType.MESH
F32 = jnp.float32
BF16 = jnp.bfloat16


def dot(a, b, dims=((1,), (0,))):
    return lax.dot_general(a, b, (dims, ((), ())), preferred_element_type=F32)


def tile_of(size):
    return 256 if size % 256 == 0 else 128


def kernel(
    owners, groups, cap,
    tok_hbm, cot_hbm, ids, gates, wg_hbm, wu_hbm, wd_hbm,
    output, grad_input, x_cols, z_cols, hid_all, dg_all, du_all,
    tokens, cotangent, wg, wu, wd, x_send, z_send, x_rows, z_rows, out_send, dx_send, out_back, dx_back,
    hid, dg, du, gate_pre, up_pre, sel, gate_hi, gate_lo,
    w_sem, self_sem, own_sem,
    x_ss, x_rs, z_ss, z_rs, o_ss, o_rs, d_ss, d_rs,
    c_ss, c_rs,
):
    me = lax.axis_index("expert")
    my_dp = lax.axis_index("dp")
    toks, width = tokens.shape
    slots = owners * cap
    hidden_units = hid.shape[1]
    cols = width // groups

    loads = [
        pltpu.make_async_copy(src, dst, w_sem.at[i])
        for i, (src, dst) in enumerate(
            (
                (tok_hbm, tokens),
                (cot_hbm, cotangent),
                (wg_hbm, wg),
                (wu_hbm, wu),
                (wd_hbm, wd),
            )
        )
    ]
    for load in loads:
        load.start()

    barrier = pltpu.get_barrier_semaphore()
    for i in range(1, owners):
        pl.semaphore_signal(
            barrier, inc=1, device_id={"expert": lax.rem(me + i, owners)}, device_id_type=MESH
        )
    for i in range(1, groups):
        pl.semaphore_signal(
            barrier, inc=1, device_id={"dp": lax.rem(my_dp + i, groups)}, device_id_type=MESH
        )

    lanes = 128
    expert = lax.broadcasted_iota(jnp.int32, (lanes, toks), 0)
    present = jnp.zeros((lanes, toks), F32)
    gate = jnp.zeros((lanes, toks), F32)
    for k in range(ids.shape[0]):
        hit = ids[k : k + 1, :] == expert
        present = jnp.where(hit, 1.0, present)
        gate = jnp.where(hit, gates[k : k + 1, :], gate)
    row = lax.broadcasted_iota(jnp.int32, (toks, toks), 0)
    col = lax.broadcasted_iota(jnp.int32, (toks, toks), 1)
    before = jnp.where(row < col, 1.0, 0.0).astype(BF16)
    rank = dot(present.astype(BF16), before)
    rank = jnp.where(present > 0.0, rank, -1.0)
    spread = jnp.where(
        lax.broadcasted_iota(jnp.int32, (slots, lanes), 0) // cap
        == lax.broadcasted_iota(jnp.int32, (slots, lanes), 1),
        1.0,
        0.0,
    ).astype(BF16)
    rank_at = dot(spread, rank.astype(BF16))
    place = lax.rem(lax.broadcasted_iota(jnp.int32, (slots, toks), 0), cap).astype(F32)
    chosen = jnp.where(rank_at == place, 1.0, 0.0)
    hi = gate.astype(BF16)
    lo = (gate - hi.astype(F32)).astype(BF16)
    hi_at = dot(spread, hi) * chosen
    lo_at = dot(spread, lo) * chosen
    sel_t = chosen.astype(BF16)
    hi_t = hi_at.astype(BF16)
    lo_t = lo_at.astype(BF16)
    dt = tile_of(width)

    loads[0].wait()

    @pl.loop(0, width // dt)
    def _(i):
        at = pl.ds(pl.multiple_of(i * dt, dt), dt)
        x_send[:, at] = dot(sel_t, tokens[:, at]).astype(BF16)

    def block(r):
        return pl.ds(pl.multiple_of(r * cap, cap), cap)

    half = owners // 2
    side, spot = me // half, lax.rem(me, half)
    near_peers = [side * half + lax.rem(spot + i, half) for i in range(1, half)]
    far_peers = [(1 - side) * half + lax.rem(spot + i, half) for i in range(half)]

    def exchange(src, dst, ss, rs, own):
        copies = [pltpu.make_async_copy(src.at[block(me), :], dst.at[block(me), :], own)]
        for i, peer in enumerate(near_peers + far_peers):
            copies.append(
                pltpu.make_async_remote_copy(
                    src_ref=src.at[block(peer), :],
                    dst_ref=dst.at[block(me), :],
                    send_sem=ss.at[i],
                    recv_sem=rs.at[i],
                    device_id={"expert": peer},
                    device_id_type=MESH,
                )
            )
        return copies[:half], copies[half:]

    def start(copies):
        for c in copies:
            c.start()

    def share(n, src_of, dst, rows):
        copies = [
            pltpu.make_async_copy(src_of(my_dp, rows), dst.at[my_dp, rows, :], own_sem.at[n])
        ]
        for i in range(1, groups):
            peer = lax.rem(my_dp + i, groups)
            copies.append(
                pltpu.make_async_remote_copy(
                    src_ref=src_of(peer, rows),
                    dst_ref=dst.at[my_dp, rows, :],
                    send_sem=c_ss.at[n, i - 1],
                    recv_sem=c_rs.at[n, i - 1],
                    device_id={"dp": peer},
                    device_id_type=MESH,
                )
            )
        start(copies)
        return copies

    def finish(copies):
        for c in copies:
            c.wait()

    def columns(ref):
        return lambda g, rows: ref.at[rows, pl.ds(pl.multiple_of(g * cols, cols), cols)]

    def whole(ref):
        return lambda g, rows: ref.at[rows, :]

    pl.semaphore_wait(barrier, owners + groups - 2)
    x_copies = exchange(x_send, x_rows, x_ss, x_rs, self_sem.at[0])
    z_copies = exchange(z_send, z_rows, z_ss, z_rs, self_sem.at[1])
    o_copies = exchange(out_send, out_back, o_ss, o_rs, self_sem.at[2])
    d_copies = exchange(dx_send, dx_back, d_ss, d_rs, self_sem.at[3])
    start(x_copies[0] + x_copies[1])

    loads[1].wait()

    @pl.loop(0, width // dt)
    def _(i):
        at = pl.ds(pl.multiple_of(i * dt, dt), dt)
        c = cotangent[:, at]
        z_send[:, at] = (dot(hi_t, c) + dot(lo_t, c)).astype(BF16)

    start(z_copies[0] + z_copies[1])
    sel[...] = chosen.T.astype(BF16)
    gate_hi[...] = hi_at.T.astype(BF16)
    gate_lo[...] = lo_at.T.astype(BF16)
    finish(loads[2:])
    ft = tile_of(hidden_units)
    part = slots // 2
    shared = []

    def forward(n, rows):
        finish(x_copies[n])
        shared.extend(share(5 * n, columns(x_rows), x_cols, rows))

        @pl.loop(0, hidden_units // ft)
        def _(i):
            at = pl.ds(pl.multiple_of(i * ft, ft), ft)
            g = dot(x_rows[rows, :], wg[:, at])
            u = dot(x_rows[rows, :], wu[:, at])
            gate_pre[rows, at] = g
            up_pre[rows, at] = u
            hid[rows, at] = (g * lax.logistic(g) * u).astype(BF16)

        shared.extend(share(5 * n + 1, whole(hid), hid_all, rows))

        @pl.loop(0, width // dt)
        def _(i):
            at = pl.ds(pl.multiple_of(i * dt, dt), dt)
            out_send[rows, at] = dot(hid[rows, :], wd[at, :], ((1,), (1,))).astype(BF16)

        start(o_copies[n])

    def backward(n, rows):
        finish(z_copies[n])
        shared.extend(share(5 * n + 2, columns(z_rows), z_cols, rows))

        @pl.loop(0, hidden_units // ft)
        def _(i):
            at = pl.ds(pl.multiple_of(i * ft, ft), ft)
            dh = dot(z_rows[rows, :], wd[:, at])
            g = gate_pre[rows, at]
            s = lax.logistic(g)
            dg[rows, at] = (dh * up_pre[rows, at] * s * (1.0 + g * (1.0 - s))).astype(BF16)
            du[rows, at] = (dh * g * s).astype(BF16)

        shared.extend(share(5 * n + 3, whole(dg), dg_all, rows))
        shared.extend(share(5 * n + 4, whole(du), du_all, rows))

        @pl.loop(0, width // dt)
        def _(i):
            at = pl.ds(pl.multiple_of(i * dt, dt), dt)
            dx_send[rows, at] = (
                dot(dg[rows, :], wg[at, :], ((1,), (1,)))
                + dot(du[rows, :], wu[at, :], ((1,), (1,)))
            ).astype(BF16)

        start(d_copies[n])

    near = pl.ds(pl.multiple_of(side * part, part), part)
    far = pl.ds(pl.multiple_of((1 - side) * part, part), part)
    forward(0, near)
    backward(0, near)
    forward(1, far)
    backward(1, far)

    finish(o_copies[0] + o_copies[1])

    @pl.loop(0, width // dt)
    def _(i):
        at = pl.ds(pl.multiple_of(i * dt, dt), dt)
        r = out_back[:, at]
        output[:, at] = (dot(gate_hi[...], r) + dot(gate_lo[...], r)).astype(BF16)

    finish(d_copies[0] + d_copies[1])

    @pl.loop(0, width // dt)
    def _(i):
        at = pl.ds(pl.multiple_of(i * dt, dt), dt)
        grad_input[:, at] = dot(sel[...], dx_back[:, at]).astype(BF16)

    finish(shared)


def weight_grads(
    out_in, dx_in, x_in, z_in, dg_in, du_in, hid_in,
    out, dx, grad_gate, grad_up, grad_down,
    out_at, dx_at, x, z, dg, du, hid, panel_gate, panel_up, panel_down, in_sem, out_sem,
):
    loads = [
        pltpu.make_async_copy(a, b, in_sem.at[i])
        for i, (a, b) in enumerate(
            (
                (x_in, x),
                (dg_in, dg),
                (du_in, du),
                (z_in, z),
                (hid_in, hid),
                (out_in, out_at),
                (dx_in, dx_at),
            )
        )
    ]
    stores = [
        pltpu.make_async_copy(a, b, out_sem.at[i])
        for i, (a, b) in enumerate(
            (
                (out_at, out),
                (dx_at, dx),
                (panel_gate, grad_gate),
                (panel_up, grad_up),
                (panel_down, grad_down),
            )
        )
    ]
    for c in loads:
        c.start()
    cols, units = x.shape[1], dg.shape[1]
    lines = units // 128
    ft = tile_of(units)
    for n, (a, b, panel, needs) in enumerate(
        (
            (x, dg, panel_gate, loads[:2]),
            (x, du, panel_up, loads[2:3]),
            (z, hid, panel_down, loads[3:5]),
        )
    ):
        for c in needs:
            c.wait()
        for f in range(0, units, ft):
            total = dot(a[...], b[:, f : f + ft], ((0,), (0,)))
            for j in range(ft // 128):
                panel[pl.ds(f // 128 + j, cols, stride=lines), :] = total[
                    :, j * 128 : (j + 1) * 128
                ]
        stores[2 + n].start()
    for load, c in zip(loads[5:], stores):
        load.wait()
        c.start()
    for c in stores:
        c.wait()


def per_device(tokens, cotangent, expert_ids, gate_values, w_gate, w_up, w_down):
    owners = lax.axis_size("expert")
    groups = lax.axis_size("dp")
    toks, width = tokens.shape
    cap = toks // 4
    local, units = w_gate.shape[1:]
    assert local == 1
    slots = owners * cap
    cols = width // groups
    vmem = pl.BlockSpec(memory_space=pltpu.VMEM)
    hbm = pl.BlockSpec(memory_space=pl.ANY)
    rows = pltpu.VMEM((slots, width), BF16)
    acts = pltpu.VMEM((slots, units), BF16)
    weight = pltpu.VMEM((width, units), BF16)
    wide = pltpu.VMEM((slots, units), F32)
    table = pltpu.VMEM((toks, slots), BF16)
    dma = pltpu.SemaphoreType.DMA
    out, dx, x_cols, z_cols, hid, dg, du = pl.pallas_call(
        functools.partial(kernel, owners, groups, cap),
        out_shape=[jax.ShapeDtypeStruct((toks, width), BF16)] * 2
        + [jax.ShapeDtypeStruct((groups, slots, cols), BF16)] * 2
        + [jax.ShapeDtypeStruct((groups, slots, units), BF16)] * 3,
        in_specs=[hbm] * 2 + [vmem] * 2 + [hbm] * 3,
        out_specs=[vmem] * 2 + [hbm] * 5,
        scratch_shapes=[pltpu.VMEM((toks, width), BF16)] * 2
        + [weight] * 3
        + [rows] * 8
        + [acts] * 3
        + [wide] * 2
        + [table] * 3
        + [dma((5,)), dma((4,)), dma((10,))]
        + [dma((owners - 1,))] * 8
        + [dma((10, groups - 1))] * 2,
        compiler_params=pltpu.CompilerParams(
            collective_id=0, has_side_effects=True, vmem_limit_bytes=58 * 2**20
        ),
        name="moe",
    )(
        tokens, cotangent, expert_ids.T, gate_values.T,
        w_gate[:, 0], w_up[:, 0], w_down[:, 0],
    )

    flat = [a.reshape(groups * slots, -1) for a in (x_cols, z_cols, dg, du, hid)]
    lines = units // 128
    panel = jax.ShapeDtypeStruct((cols * lines, 128), F32)
    out, dx, *panels = pl.pallas_call(
        weight_grads,
        out_shape=[jax.ShapeDtypeStruct((toks, width), BF16)] * 2 + [panel] * 3,
        in_specs=[hbm] * 7,
        out_specs=[hbm] * 5,
        scratch_shapes=[pltpu.VMEM(a.shape, BF16) for a in (out, dx, *flat)]
        + [pltpu.VMEM(panel.shape, F32)] * 3
        + [dma((7,)), dma((5,))],
        compiler_params=pltpu.CompilerParams(vmem_limit_bytes=58 * 2**20),
        name="weight_grads",
    )(out, dx, *flat)
    return out, dx, *(p.reshape(cols, 1, units) for p in panels)


def solution(mesh):
    rows = P(("dp", "expert"), None)
    held = P(None, "expert", None)
    grads = P("dp", "expert", None)
    return jax.shard_map(
        per_device,
        mesh=mesh,
        in_specs=(rows, rows, rows, rows, held, held, held),
        out_specs=(rows, rows, grads, grads, grads),
        check_vma=False,
    )
```

```python
import functools

import jax
import jax.numpy as jnp
from jax import lax
from jax.experimental import pallas as pl
from jax.experimental.pallas import tpu as pltpu
from jax.sharding import PartitionSpec as P

MESH = pl.DeviceIdType.MESH
F32 = jnp.float32
BF16 = jnp.bfloat16


def dot(a, b, dims=((1,), (0,))):
    return lax.dot_general(a, b, (dims, ((), ())), preferred_element_type=F32)


def tile_of(size):
    return 512 if size % 512 == 0 else 384 if size % 384 == 0 else 128


def kernel(
    owners, groups, cap,
    tok_hbm, cot_hbm, ids, gates, wg_hbm, wu_hbm, wd_hbm,
    output, grad_input, x_cols, z_cols, hid_all, dg_all, du_all,
    tokens, cotangent, wg, wu, wd, x_send, z_send, x_rows, z_rows, out_send, dx_send, out_back, dx_back,
    hid, dg, du, gate_pre, up_pre, sel, gate_hi, gate_lo,
    w_sem, self_sem, own_sem,
    x_ss, x_rs, z_ss, z_rs, o_ss, o_rs, d_ss, d_rs,
    c_ss, c_rs,
):
    me = lax.axis_index("expert")
    my_dp = lax.axis_index("dp")
    toks, width = tokens.shape
    slots = owners * cap
    hidden_units = hid.shape[1]
    cols = width // groups

    loads = [
        pltpu.make_async_copy(src, dst, w_sem.at[i])
        for i, (src, dst) in enumerate(
            (
                (tok_hbm, tokens),
                (cot_hbm, cotangent),
                (wg_hbm, wg),
                (wu_hbm, wu),
                (wd_hbm, wd),
            )
        )
    ]
    for load in loads:
        load.start()

    barrier = pltpu.get_barrier_semaphore()
    for i in range(1, owners):
        pl.semaphore_signal(
            barrier, inc=1, device_id={"expert": lax.rem(me + i, owners)}, device_id_type=MESH
        )
    for i in range(1, groups):
        pl.semaphore_signal(
            barrier, inc=1, device_id={"dp": lax.rem(my_dp + i, groups)}, device_id_type=MESH
        )

    lanes = 128
    expert = lax.broadcasted_iota(jnp.int32, (lanes, toks), 0)
    present = jnp.zeros((lanes, toks), F32)
    gate = jnp.zeros((lanes, toks), F32)
    for k in range(ids.shape[0]):
        hit = ids[k : k + 1, :] == expert
        present = jnp.where(hit, 1.0, present)
        gate = jnp.where(hit, gates[k : k + 1, :], gate)
    row = lax.broadcasted_iota(jnp.int32, (toks, toks), 0)
    col = lax.broadcasted_iota(jnp.int32, (toks, toks), 1)
    before = jnp.where(row < col, 1.0, 0.0).astype(BF16)
    rank = dot(present.astype(BF16), before)
    rank = jnp.where(present > 0.0, rank, -1.0)
    spread = jnp.where(
        lax.broadcasted_iota(jnp.int32, (slots, lanes), 0) // cap
        == lax.broadcasted_iota(jnp.int32, (slots, lanes), 1),
        1.0,
        0.0,
    ).astype(BF16)
    rank_at = dot(spread, rank.astype(BF16))
    place = lax.rem(lax.broadcasted_iota(jnp.int32, (slots, toks), 0), cap).astype(F32)
    chosen = jnp.where(rank_at == place, 1.0, 0.0)
    hi = gate.astype(BF16)
    lo = (gate - hi.astype(F32)).astype(BF16)
    hi_at = dot(spread, hi) * chosen
    lo_at = dot(spread, lo) * chosen
    sel_t = chosen.astype(BF16)
    hi_t = hi_at.astype(BF16)
    lo_t = lo_at.astype(BF16)
    dt = tile_of(width)

    loads[0].wait()

    @pl.loop(0, width // dt)
    def _(i):
        at = pl.ds(pl.multiple_of(i * dt, dt), dt)
        x_send[:, at] = dot(sel_t, tokens[:, at]).astype(BF16)

    def block(r):
        return pl.ds(pl.multiple_of(r * cap, cap), cap)

    half = owners // 2
    side, spot = me // half, lax.rem(me, half)
    near_peers = [side * half + lax.rem(spot + i, half) for i in range(1, half)]
    far_peers = [(1 - side) * half + lax.rem(spot + i, half) for i in range(half)]

    def exchange(src, dst, ss, rs, own):
        copies = [pltpu.make_async_copy(src.at[block(me), :], dst.at[block(me), :], own)]
        for i, peer in enumerate(near_peers + far_peers):
            copies.append(
                pltpu.make_async_remote_copy(
                    src_ref=src.at[block(peer), :],
                    dst_ref=dst.at[block(me), :],
                    send_sem=ss.at[i],
                    recv_sem=rs.at[i],
                    device_id={"expert": peer},
                    device_id_type=MESH,
                )
            )
        return copies[:half], copies[half:]

    def start(copies):
        for c in copies:
            c.start()

    def share(n, src_of, dst, rows):
        copies = [
            pltpu.make_async_copy(src_of(my_dp, rows), dst.at[my_dp, rows, :], own_sem.at[n])
        ]
        for i in range(1, groups):
            peer = lax.rem(my_dp + i, groups)
            copies.append(
                pltpu.make_async_remote_copy(
                    src_ref=src_of(peer, rows),
                    dst_ref=dst.at[my_dp, rows, :],
                    send_sem=c_ss.at[n, i - 1],
                    recv_sem=c_rs.at[n, i - 1],
                    device_id={"dp": peer},
                    device_id_type=MESH,
                )
            )
        start(copies)
        return copies

    def finish(copies):
        for c in copies:
            c.wait()

    def columns(ref):
        return lambda g, rows: ref.at[rows, pl.ds(pl.multiple_of(g * cols, cols), cols)]

    def whole(ref):
        return lambda g, rows: ref.at[rows, :]

    pl.semaphore_wait(barrier, owners + groups - 2)
    x_copies = exchange(x_send, x_rows, x_ss, x_rs, self_sem.at[0])
    z_copies = exchange(z_send, z_rows, z_ss, z_rs, self_sem.at[1])
    o_copies = exchange(out_send, out_back, o_ss, o_rs, self_sem.at[2])
    d_copies = exchange(dx_send, dx_back, d_ss, d_rs, self_sem.at[3])
    start(x_copies[0] + x_copies[1])

    loads[1].wait()

    @pl.loop(0, width // dt)
    def _(i):
        at = pl.ds(pl.multiple_of(i * dt, dt), dt)
        c = cotangent[:, at]
        z_send[:, at] = (dot(hi_t, c) + dot(lo_t, c)).astype(BF16)

    start(z_copies[0] + z_copies[1])
    sel[...] = chosen.T.astype(BF16)
    gate_hi[...] = hi_at.T.astype(BF16)
    gate_lo[...] = lo_at.T.astype(BF16)
    finish(loads[2:])
    ft = tile_of(hidden_units)
    part = slots // 2
    shared = []

    def forward(n, rows):
        finish(x_copies[n])
        shared.extend(share(5 * n, columns(x_rows), x_cols, rows))

        @pl.loop(0, hidden_units // ft)
        def _(i):
            at = pl.ds(pl.multiple_of(i * ft, ft), ft)
            g = dot(x_rows[rows, :], wg[:, at])
            u = dot(x_rows[rows, :], wu[:, at])
            gate_pre[rows, at] = g
            up_pre[rows, at] = u
            hid[rows, at] = (g * lax.logistic(g) * u).astype(BF16)

        shared.extend(share(5 * n + 1, whole(hid), hid_all, rows))

        @pl.loop(0, width // dt)
        def _(i):
            at = pl.ds(pl.multiple_of(i * dt, dt), dt)
            out_send[rows, at] = dot(hid[rows, :], wd[at, :], ((1,), (1,))).astype(BF16)

        start(o_copies[n])

    def backward(n, rows):
        finish(z_copies[n])
        shared.extend(share(5 * n + 2, columns(z_rows), z_cols, rows))

        @pl.loop(0, hidden_units // ft)
        def _(i):
            at = pl.ds(pl.multiple_of(i * ft, ft), ft)
            dh = dot(z_rows[rows, :], wd[:, at])
            g = gate_pre[rows, at]
            s = lax.logistic(g)
            dg[rows, at] = (dh * up_pre[rows, at] * s * (1.0 + g * (1.0 - s))).astype(BF16)
            du[rows, at] = (dh * g * s).astype(BF16)

        shared.extend(share(5 * n + 3, whole(dg), dg_all, rows))
        shared.extend(share(5 * n + 4, whole(du), du_all, rows))

        @pl.loop(0, width // dt)
        def _(i):
            at = pl.ds(pl.multiple_of(i * dt, dt), dt)
            dx_send[rows, at] = (
                dot(dg[rows, :], wg[at, :], ((1,), (1,)))
                + dot(du[rows, :], wu[at, :], ((1,), (1,)))
            ).astype(BF16)

        start(d_copies[n])

    near = pl.ds(pl.multiple_of(side * part, part), part)
    far = pl.ds(pl.multiple_of((1 - side) * part, part), part)
    forward(0, near)
    forward(1, far)
    backward(0, near)
    backward(1, far)

    finish(o_copies[0] + o_copies[1])

    @pl.loop(0, width // dt)
    def _(i):
        at = pl.ds(pl.multiple_of(i * dt, dt), dt)
        r = out_back[:, at]
        output[:, at] = (dot(gate_hi[...], r) + dot(gate_lo[...], r)).astype(BF16)

    finish(d_copies[0] + d_copies[1])

    @pl.loop(0, width // dt)
    def _(i):
        at = pl.ds(pl.multiple_of(i * dt, dt), dt)
        grad_input[:, at] = dot(sel[...], dx_back[:, at]).astype(BF16)

    finish(shared)


def weight_grads(
    out_in, dx_in, x_in, z_in, dg_in, du_in, hid_in,
    out, dx, grad_gate, grad_up, grad_down,
    out_at, dx_at, x, z, dg, du, hid, panel_gate, panel_up, panel_down, in_sem, out_sem,
):
    loads = [
        pltpu.make_async_copy(a, b, in_sem.at[i])
        for i, (a, b) in enumerate(
            (
                (x_in, x),
                (dg_in, dg),
                (du_in, du),
                (z_in, z),
                (hid_in, hid),
                (out_in, out_at),
                (dx_in, dx_at),
            )
        )
    ]
    stores = [
        pltpu.make_async_copy(a, b, out_sem.at[i])
        for i, (a, b) in enumerate(
            (
                (out_at, out),
                (dx_at, dx),
                (panel_gate, grad_gate),
                (panel_up, grad_up),
                (panel_down, grad_down),
            )
        )
    ]
    for c in loads:
        c.start()
    cols, units = x.shape[1], dg.shape[1]
    lines = units // 128
    ft = tile_of(units)
    for n, (a, b, panel, needs) in enumerate(
        (
            (x, dg, panel_gate, loads[:2]),
            (x, du, panel_up, loads[2:3]),
            (z, hid, panel_down, loads[3:5]),
        )
    ):
        for c in needs:
            c.wait()
        for f in range(0, units, ft):
            total = dot(a[...], b[:, f : f + ft], ((0,), (0,)))
            for j in range(ft // 128):
                panel[pl.ds(f // 128 + j, cols, stride=lines), :] = total[
                    :, j * 128 : (j + 1) * 128
                ]
        stores[2 + n].start()
    for load, c in zip(loads[5:], stores):
        load.wait()
        c.start()
    for c in stores:
        c.wait()


def per_device(tokens, cotangent, expert_ids, gate_values, w_gate, w_up, w_down):
    owners = lax.axis_size("expert")
    groups = lax.axis_size("dp")
    toks, width = tokens.shape
    cap = toks // 4
    local, units = w_gate.shape[1:]
    assert local == 1
    slots = owners * cap
    cols = width // groups
    vmem = pl.BlockSpec(memory_space=pltpu.VMEM)
    hbm = pl.BlockSpec(memory_space=pl.ANY)
    rows = pltpu.VMEM((slots, width), BF16)
    acts = pltpu.VMEM((slots, units), BF16)
    weight = pltpu.VMEM((width, units), BF16)
    wide = pltpu.VMEM((slots, units), F32)
    table = pltpu.VMEM((toks, slots), BF16)
    dma = pltpu.SemaphoreType.DMA
    out, dx, x_cols, z_cols, hid, dg, du = pl.pallas_call(
        functools.partial(kernel, owners, groups, cap),
        out_shape=[jax.ShapeDtypeStruct((toks, width), BF16)] * 2
        + [jax.ShapeDtypeStruct((groups, slots, cols), BF16)] * 2
        + [jax.ShapeDtypeStruct((groups, slots, units), BF16)] * 3,
        in_specs=[hbm] * 2 + [vmem] * 2 + [hbm] * 3,
        out_specs=[vmem] * 2 + [hbm] * 5,
        scratch_shapes=[pltpu.VMEM((toks, width), BF16)] * 2
        + [weight] * 3
        + [rows] * 8
        + [acts] * 3
        + [wide] * 2
        + [table] * 3
        + [dma((5,)), dma((4,)), dma((10,))]
        + [dma((owners - 1,))] * 8
        + [dma((10, groups - 1))] * 2,
        compiler_params=pltpu.CompilerParams(
            collective_id=0, has_side_effects=True, vmem_limit_bytes=58 * 2**20
        ),
        name="moe",
    )(
        tokens, cotangent, expert_ids.T, gate_values.T,
        w_gate[:, 0], w_up[:, 0], w_down[:, 0],
    )

    flat = [a.reshape(groups * slots, -1) for a in (x_cols, z_cols, dg, du, hid)]
    lines = units // 128
    panel = jax.ShapeDtypeStruct((cols * lines, 128), F32)
    out, dx, *panels = pl.pallas_call(
        weight_grads,
        out_shape=[jax.ShapeDtypeStruct((toks, width), BF16)] * 2 + [panel] * 3,
        in_specs=[hbm] * 7,
        out_specs=[hbm] * 5,
        scratch_shapes=[pltpu.VMEM(a.shape, BF16) for a in (out, dx, *flat)]
        + [pltpu.VMEM(panel.shape, F32)] * 3
        + [dma((7,)), dma((5,))],
        compiler_params=pltpu.CompilerParams(vmem_limit_bytes=58 * 2**20),
        name="weight_grads",
    )(out, dx, *flat)
    return out, dx, *(p.reshape(cols, 1, units) for p in panels)


def solution(mesh):
    rows = P(("dp", "expert"), None)
    held = P(None, "expert", None)
    grads = P("dp", "expert", None)
    return jax.shard_map(
        per_device,
        mesh=mesh,
        in_specs=(rows, rows, rows, rows, held, held, held),
        out_specs=(rows, rows, grads, grads, grads),
        check_vma=False,
    )
```
